512 devices in a mesh: blk: 128 (over x_hi, y, z), grp: 4 (over x_lo, core).
Axes of the slice: x: 4 (x_hi: 2, x_lo: 2; x = x_hi * 2 + x_lo), y: 4, z: 16, core: 2. Of those that a mesh axis runs over, the one named last changes fastest.
Arguments:
- image_emb: bfloat16 [196608, 1152], P(('blk', 'grp')), may hold values from -0.1875 to 0.1875
- text_emb: bfloat16 [196608, 1152], P(('blk', 'grp')), may hold values from -0.1875 to 0.1875
- positives: int32 [512, 384], P(('blk', 'grp')), may hold values from 0 to 383, each once within a row
- pair_mask: int32 [128, 7], replicated, may hold values from 0 to 1, as said below
- log_scale: float32 [1], replicated, may hold values from 1.5 to 2.5
- bias: float32 [1], replicated, may hold values from -3 to -1
Outputs:
- image_grad: bfloat16 [196608, 1152], P(('blk', 'grp'))
- text_grad: bfloat16 [196608, 1152], P(('blk', 'grp'))
- loss: float32 [1], replicated
The draws below stay inside these ranges and needn't reach their ends.
Inputs may be any that keep to these rules, and one draw needn't show every extreme that they name: `positives`: every row is a permutation of the rows of a block. `pair_mask`: column 3 is 1 in every row (each image block is scored against its own text block); at least one row is all ones.
All inputs are finite; a program needn't handle non-finite values.
Results may differ from the reference program's by a relative error of at most 0.0063.
Values may be sent and summed in bfloat16 or wider, within the bound.
No kernel may reach another device: no remote copies, remote signals or barrier semaphores. Data moves between devices by JAX's collectives and lax.ppermute only.
A program may use at most 64 MiB of HBM per device.

```python
import jax
import jax.numpy as jnp
from jax import lax

D = 1152
ROWS = 384
REACH = 3
IMAGES = 196608
N_BLK = 128
N_GRP = 4


def draw_pair_mask(key, part):
    first_key = jax.random.fold_in(key, 11)
    second_key = jax.random.fold_in(key, 23)
    coins = jax.random.randint(first_key, (N_BLK, 2 * REACH + 1), 0, 4)
    chosen = jnp.where(coins == 0, 1, 0).astype(jnp.int32)
    full_row = jax.random.randint(second_key, (), 0, N_BLK)
    row_index = lax.broadcasted_iota(jnp.int32, (N_BLK, 2 * REACH + 1), 0)
    col_index = lax.broadcasted_iota(jnp.int32, (N_BLK, 2 * REACH + 1), 1)
    chosen = jnp.where(row_index == full_row, 1, chosen)
    chosen = jnp.where(col_index == REACH, 1, chosen)
    return chosen.astype(jnp.int32)


def shard_levels(key, shape, pieces, least, high):
    level, own = 1.0, jax.random.fold_in(key, 6)
    for position, blocks in pieces:
        steps = jnp.exp(jax.random.uniform(jax.random.fold_in(own, position), (blocks,), jnp.float32, least / len(pieces), high / len(pieces)))
        level = level * jnp.repeat(steps, shape[position] // blocks).reshape([-1 if axis == position else 1 for axis in range(len(shape))])
    return level


def centred(own_key, dims, width, limit, shards=(), dtype=jnp.bfloat16):
    array = jax.random.normal(own_key, dims, jnp.float32) * width
    if len(shards) > 0:
        array = shard_levels(own_key, dims, shards, -0.22, 0.18) * array
    return jnp.clip(array, min=-limit, max=limit).astype(dtype)


def setup_inputs(seed: int = 0) -> dict:
    splits = jax.random.split(jax.random.key(seed), 7)
    image_emb = centred(splits[0], (IMAGES, D), D ** -0.5, 0.1875, ((0, 512),))
    text_emb = centred(splits[1], (IMAGES, D), D ** -0.5, 0.1875, ((0, 512),))
    positives = jax.vmap(lambda own: jax.random.permutation(own, ROWS))(jax.random.split(splits[2], (N_BLK * N_GRP))).reshape((N_BLK * N_GRP, ROWS)).astype(jnp.int32)
    pair_mask = draw_pair_mask(jax.random.fold_in(splits[6], 71), 0)
    log_scale = jnp.clip(jax.random.uniform(splits[4], (1,), jnp.float32, 1.5, 2.5), 1.5, 2.5)
    bias = jnp.clip(jax.random.uniform(splits[5], (1,), jnp.float32, -3.0, -1.0), -3.0, -1.0)
    return {"image_emb": image_emb, "text_emb": text_emb, "positives": positives, "pair_mask": pair_mask, "log_scale": log_scale, "bias": bias}


epsilon = 1e-06

def unit_rows(embedded):
    values = embedded.astype(jnp.float32)
    length = jnp.sqrt(lax.optimization_barrier(jnp.sum(values * values, axis=1, keepdims=True)) + epsilon)
    return (values / length, length)

def back_rows(normed, length, upstream):
    inward = lax.optimization_barrier(jnp.sum(normed * upstream, axis=1, keepdims=True))
    return (upstream - normed * inward) / length

def score_tile(image_side, text_side, labels, logit_scale, offset):
    similar = jnp.einsum('rd,cd->rc', image_side, text_side, preferred_element_type=jnp.float32)
    logits = logit_scale * similar + offset
    signed = labels * logits
    loss_sum = jnp.sum(jax.nn.softplus(-signed))
    slopes = (-labels * jax.nn.sigmoid(-signed) * logit_scale).astype(jnp.bfloat16)
    return (slopes, loss_sum)

def masked_tile(active_flag, image_side, text_side, labels, logit_scale, offset):

    def active(unused):
        return score_tile(image_side, text_side, labels, logit_scale, offset)

    def skipped(unused):
        return (jnp.zeros((image_side.shape[0], text_side.shape[0]), jnp.bfloat16), jnp.zeros((), jnp.float32))
    return lax.cond(active_flag > 0, active, skipped, 0)

def reference(image_emb, text_emb, positives, pair_mask, log_scale, bias):
    logit_scale = jnp.exp(log_scale[0])
    offset = bias[0]
    image_normed, image_len = unit_rows(image_emb)
    text_normed, text_len = unit_rows(text_emb)
    block_count = N_BLK * N_GRP
    image_blocks = image_normed.astype(jnp.bfloat16).reshape(block_count, ROWS, D)
    text_blocks = text_normed.astype(jnp.bfloat16).reshape(N_BLK, N_GRP, ROWS, D)
    columns = lax.broadcasted_iota(jnp.int32, (ROWS, ROWS), 1)
    image_total = jnp.zeros((block_count, ROWS, D), jnp.float32)
    text_total = jnp.zeros((N_BLK, N_GRP, ROWS, D), jnp.float32)
    loss_total = jnp.zeros((), jnp.float32)
    for distance in range(-REACH, REACH + 1):
        partner = jnp.roll(text_blocks, -distance, axis=0).reshape(block_count, ROWS, D)
        flags = jnp.broadcast_to(pair_mask[:, REACH + distance][:, None], (N_BLK, N_GRP)).reshape(block_count)

        def one_block(items, distance=distance):
            image_side, text_side, active_flag, matches = items
            if distance == 0:
                labels = jnp.where(matches[:, None] == columns, 1.0, -1.0).astype(jnp.float32)
            else:
                labels = -jnp.ones((ROWS, ROWS), jnp.float32)
            slopes, part_loss = masked_tile(active_flag, image_side, text_side, labels, logit_scale, offset)
            image_part = jnp.dot(slopes, text_side, preferred_element_type=jnp.float32)
            text_part = jnp.einsum('rc,rd->cd', slopes, image_side, preferred_element_type=jnp.float32)
            if distance != 0:
                text_part = lax.optimization_barrier(text_part.astype(jnp.bfloat16)).astype(jnp.float32)
            return (image_part, text_part, part_loss)
        image_part, text_part, parts = lax.map(one_block, (image_blocks, partner, flags, positives))
        image_total = image_total + image_part
        text_total = text_total + jnp.roll(text_part.reshape(N_BLK, N_GRP, ROWS, D), distance, axis=0)
        loss_total = loss_total + jnp.sum(parts)
    image_grad = back_rows(image_normed, image_len, image_total.reshape(IMAGES, D)).astype(jnp.bfloat16)
    text_grad = back_rows(text_normed, text_len, text_total.reshape(IMAGES, D)).astype(jnp.bfloat16)
    loss = (loss_total / IMAGES).reshape(1)
    return (image_grad, text_grad, loss)
```

```python
import functools

import jax
import jax.numpy as jnp
from jax import lax
from jax.experimental import pallas as pl
from jax.experimental.pallas import tpu as pltpu
from jax.sharding import Mesh
from jax.sharding import PartitionSpec as P

ALL = ("x_hi", "y", "z", "x_lo", "core")
BLK = ("x_hi", "y", "z")

EPSILON = 1e-06
VMEM_LIMIT = 32 * 1024 * 1024


def shifted(value, axis, steps):
    count = lax.axis_size(axis)
    return lax.ppermute(value, axis, [(s, (s + steps) % count) for s in range(count)])


def dot(a, b, contract):
    return lax.dot_general(a, b, ((contract[:1], contract[1:]), ((), ())), preferred_element_type=jnp.float32)


def unit_of(raw):
    values = raw.astype(jnp.float32)
    inverse = lax.rsqrt(jnp.sum(values * values, axis=1, keepdims=True) + EPSILON)
    return values * inverse, inverse


def loss_and_sigmoid(u):
    small = jnp.exp(-jnp.abs(u))
    loss = jnp.maximum(u, 0.0) + jnp.log1p(small)
    return loss, jnp.where(u >= 0.0, 1.0, small) / (1.0 + small)


def own_kernel(scal, positives, image, text, image_half, text_half, image_acc, text_acc, loss):
    image_half[...] = unit_of(image[...])[0].astype(jnp.bfloat16)
    text_half[...] = unit_of(text[...])[0].astype(jnp.bfloat16)
    z = scal[0] * dot(text_half[...], image_half[...], (1, 1)) + scal[1]
    match = lax.broadcasted_iota(jnp.int32, z.shape, 0) == positives[...]
    part, sigmoid = loss_and_sigmoid(jnp.where(match, -z, z))
    loss[0] = jnp.sum(part)
    slopes = (jnp.where(match, -sigmoid, sigmoid) * scal[0]).astype(jnp.bfloat16)
    text_acc[...] = dot(slopes, image_half[...], (1, 0))
    image_acc[...] = dot(slopes, text_half[...], (0, 0))


def pair_kernel(which, with_loss, last, flags, scal, *refs):
    refs = list(refs)
    loss_in = refs.pop(0) if with_loss else None
    half, acc = refs.pop(0), refs.pop(0)
    raw = refs.pop(0) if last else None
    partners = [refs.pop(0) for _ in which]
    out = refs.pop(0)
    loss_out = refs.pop(0) if with_loss else None
    total = refs.pop(0) if last else out
    total[...] = acc[...]
    if with_loss:
        loss_out[0] = loss_in[0]
    for (row, column), partner in zip(which, partners):

        @pl.when(flags[row, column] > 0)
        def _(partner=partner):
            other = unit_of(partner[...])[0].astype(jnp.bfloat16)
            z = scal[0] * dot(half[...], other, (1, 1)) + scal[1]
            part, sigmoid = loss_and_sigmoid(z)
            if with_loss:
                loss_out[0] = loss_out[0] + jnp.sum(part)
            slopes = (sigmoid * scal[0]).astype(jnp.bfloat16)
            total[...] += dot(slopes, other, (1, 0))

    if last:
        unit, inverse = unit_of(raw[...])
        upstream = total[...]
        inward = jnp.sum(unit * upstream, axis=1, keepdims=True)
        out[...] = ((upstream - unit * inward) * inverse).astype(jnp.bfloat16)


SMEM = pl.BlockSpec(memory_space=pltpu.SMEM)
VMEM = pl.BlockSpec(memory_space=pltpu.VMEM)


def cost(pairs, blocks):
    return pl.CostEstimate(flops=pairs * 4 * 384 * 384 * 1152, bytes_accessed=blocks * 384 * 1152 * 2, transcendentals=pairs * 3 * 384 * 384)


def own_pair(scal, positives, image, text):
    shape = image.shape
    return pl.pallas_call(
        own_kernel,
        out_shape=[jax.ShapeDtypeStruct(shape, jnp.bfloat16)] * 2 + [jax.ShapeDtypeStruct(shape, jnp.float32)] * 2 + [jax.ShapeDtypeStruct((1,), jnp.float32)],
        in_specs=[SMEM, VMEM, VMEM, VMEM],
        out_specs=[VMEM] * 4 + [SMEM],
        compiler_params=pltpu.CompilerParams(vmem_limit_bytes=VMEM_LIMIT),
        cost_estimate=cost(2, 8),
        name="own_pair",
    )(scal, positives, image, text)


def add_pairs(which, flags, scal, loss, half, acc, raw, partners, name):
    with_loss, last = loss is not None, raw is not None
    operands = [flags, scal] + ([loss] if with_loss else []) + [half, acc] + ([raw] if last else []) + list(partners)
    in_specs = [SMEM, SMEM] + ([SMEM] if with_loss else []) + [VMEM] * (2 + last + len(partners))
    out_shape = [jax.ShapeDtypeStruct(acc.shape, jnp.bfloat16 if last else jnp.float32)]
    out_specs = [VMEM]
    if with_loss:
        out_shape.append(jax.ShapeDtypeStruct((1,), jnp.float32))
        out_specs.append(SMEM)
    aliases = {} if last else {3 + with_loss: 0}
    return pl.pallas_call(
        functools.partial(pair_kernel, tuple(which), with_loss, last),
        out_shape=out_shape,
        in_specs=in_specs,
        out_specs=out_specs,
        scratch_shapes=[pltpu.VMEM(acc.shape, jnp.float32)] if last else [],
        input_output_aliases=aliases,
        compiler_params=pltpu.CompilerParams(vmem_limit_bytes=VMEM_LIMIT),
        cost_estimate=cost(len(partners), 6 + len(partners)),
        name=name,
    )(*operands)


def flags_of(pair_mask, reach):
    count = pair_mask.shape[0]
    me = lax.axis_index(BLK)
    block = lax.broadcasted_iota(jnp.int32, pair_mask.shape, 0)
    e = lax.broadcasted_iota(jnp.int32, pair_mask.shape, 1) - reach
    mine = jnp.sum(jnp.where(block == me, pair_mask, 0), axis=0)
    theirs = jnp.sum(jnp.where(block == lax.rem(me - e + count, count), pair_mask, 0), axis=0)
    return jnp.stack([mine, theirs])


def summed(value):
    for axis in ("core", "x_lo", "x_hi", "y", "z"):
        step = 1
        while step < lax.axis_size(axis):
            value = value + shifted(value, axis, step)
            step *= 2
    return value


def body(image_emb, text_emb, positives, pair_mask, log_scale, bias):
    reach = (pair_mask.shape[1] - 1) // 2
    scal = jnp.concatenate([jnp.exp(log_scale), bias])
    flags = flags_of(pair_mask, reach)

    texts, images = {0: text_emb}, {0: image_emb}
    for distance in range(1, reach + 1):
        for held in (texts, images):
            for sign in (1, -1):
                held[sign * distance] = shifted(held[sign * (distance - 1)], BLK, -sign)

    image_half, text_half, image_acc, text_acc, loss = own_pair(scal, positives, image_emb, text_emb)
    for d in range(1, reach + 1):
        last = d == reach
        image_acc, loss = add_pairs(
            [(0, reach + d), (0, reach - d)], flags, scal, loss, image_half, image_acc,
            image_emb if last else None, [texts[d], texts[-d]], f"image_side_{d}",
        )
        (text_acc,) = add_pairs(
            [(1, reach - d), (1, reach + d)], flags, scal, None, text_half, text_acc,
            text_emb if last else None, [images[d], images[-d]], f"text_side_{d}",
        )
    total = summed(loss)
    image_count = image_emb.shape[0] * lax.axis_size(ALL)
    return image_acc, text_acc, total / image_count


def solution(mesh):
    fine = Mesh(mesh.devices.reshape(2, 4, 16, 2, 2), ALL)
    rows = P(ALL, None)
    return jax.shard_map(
        body,
        mesh=fine,
        in_specs=(rows, rows, rows, P(), P(), P()),
        out_specs=(rows, rows, P()),
        check_vma=False,
    )
```

```python
import functools

import jax
import jax.numpy as jnp
from jax import lax
from jax.experimental import pallas as pl
from jax.experimental.pallas import tpu as pltpu
from jax.sharding import Mesh
from jax.sharding import PartitionSpec as P

ALL = ("x_hi", "y", "z", "x_lo", "core")
BLK = ("x_hi", "y", "z")

EPSILON = 1e-06
VMEM_LIMIT = 16 * 1024 * 1024


def shifted(value, axis, steps):
    count = lax.axis_size(axis)
    return lax.ppermute(value, axis, [(s, (s + steps) % count) for s in range(count)])


def dot(a, b, contract):
    return lax.dot_general(a, b, ((contract[:1], contract[1:]), ((), ())), preferred_element_type=jnp.float32)


def unit_of(raw):
    values = raw.astype(jnp.float32)
    inverse = lax.rsqrt(jnp.sum(values * values, axis=1, keepdims=True) + EPSILON)
    return values * inverse, inverse


def loss_and_sigmoid(u):
    small = jnp.exp(-jnp.abs(u))
    loss = jnp.maximum(u, 0.0) + jnp.log1p(small)
    return loss, jnp.where(u >= 0.0, 1.0, small) / (1.0 + small)


def grad_of(raw, upstream):
    unit, inverse = unit_of(raw)
    inward = jnp.sum(unit * upstream, axis=1, keepdims=True)
    return ((upstream - unit * inward) * inverse).astype(jnp.bfloat16)


def own_kernel(scal, positives, image, text, image_half, text_half, image_acc, text_acc, loss):
    image_half[...] = unit_of(image[...])[0].astype(jnp.bfloat16)
    text_half[...] = unit_of(text[...])[0].astype(jnp.bfloat16)
    z = scal[0] * dot(text_half[...], image_half[...], (1, 1)) + scal[1]
    match = lax.broadcasted_iota(jnp.int32, z.shape, 0) == positives[...]
    part, sigmoid = loss_and_sigmoid(jnp.where(match, -z, z))
    loss[0] = jnp.sum(part)
    slopes = (jnp.where(match, -sigmoid, sigmoid) * scal[0]).astype(jnp.bfloat16)
    text_acc[...] = dot(slopes, image_half[...], (1, 0))
    image_acc[...] = dot(slopes, text_half[...], (0, 0))


def pair_kernel(which, with_loss, last, flags, scal, *refs):
    refs = list(refs)
    loss_in = refs.pop(0) if with_loss else None
    half, acc = refs.pop(0), refs.pop(0)
    raw = refs.pop(0) if last else None
    partners = [refs.pop(0) for _ in which]
    out = refs.pop(0)
    loss_out = refs.pop(0) if with_loss else None
    total = refs.pop(0) if last else out
    loss = refs.pop(0) if with_loss and last else loss_out
    total[...] = acc[...]
    if with_loss:
        loss[0] = loss_in[0]
    for (row, column), partner in zip(which, partners):

        @pl.when(flags[row, column] > 0)
        def _(partner=partner):
            other = unit_of(partner[...])[0].astype(jnp.bfloat16)
            z = scal[0] * dot(half[...], other, (1, 1)) + scal[1]
            part, sigmoid = loss_and_sigmoid(z)
            if with_loss:
                loss[0] = loss[0] + jnp.sum(part)
            slopes = (sigmoid * scal[0]).astype(jnp.bfloat16)
            total[...] += dot(slopes, other, (1, 0))

    if last:
        out[...] = grad_of(raw[...], total[...])
        if with_loss:
            loss_out[...] = jnp.full(loss_out.shape, loss[0], jnp.float32)


def total_kernel(received, out):
    out[...] = jnp.broadcast_to(jnp.sum(received[...], axis=0, keepdims=True), out.shape)


SMEM = pl.BlockSpec(memory_space=pltpu.SMEM)
VMEM = pl.BlockSpec()


def cost(pairs, blocks):
    return pl.CostEstimate(flops=pairs * 4 * 384 * 384 * 1152, bytes_accessed=blocks * 384 * 1152 * 2, transcendentals=pairs * 3 * 384 * 384)


def own_pair(scal, positives, image, text):
    shape = image.shape
    return pl.pallas_call(
        own_kernel,
        out_shape=[jax.ShapeDtypeStruct(shape, jnp.bfloat16)] * 2 + [jax.ShapeDtypeStruct(shape, jnp.float32)] * 2 + [jax.ShapeDtypeStruct((1,), jnp.float32)],
        in_specs=[SMEM, VMEM, VMEM, VMEM],
        out_specs=[VMEM] * 4 + [SMEM],
        compiler_params=pltpu.CompilerParams(vmem_limit_bytes=VMEM_LIMIT),
        cost_estimate=cost(2, 8),
        name="own_pair",
    )(scal, positives, image, text)


def add_pairs(which, flags, scal, loss, half, acc, raw, partners, name, copies=0):
    with_loss, last = loss is not None, raw is not None
    operands = [flags, scal] + ([loss] if with_loss else []) + [half, acc] + ([raw] if last else []) + list(partners)
    in_specs = [SMEM, SMEM] + ([SMEM] if with_loss else []) + [VMEM] * (2 + last + len(partners))
    out_shape = [jax.ShapeDtypeStruct(acc.shape, jnp.bfloat16 if last else jnp.float32)]
    out_specs = [VMEM]
    if with_loss:
        out_shape.append(jax.ShapeDtypeStruct((copies, 1, 128) if last else (1,), jnp.float32))
        out_specs.append(VMEM if last else SMEM)
    aliases = {} if last else {3 + with_loss: 0}
    return pl.pallas_call(
        functools.partial(pair_kernel, tuple(which), with_loss, last),
        out_shape=out_shape,
        in_specs=in_specs,
        out_specs=out_specs,
        scratch_shapes=([pltpu.VMEM(acc.shape, jnp.float32)] + [pltpu.SMEM((1,), jnp.float32)] * with_loss) if last else [],
        input_output_aliases=aliases,
        compiler_params=pltpu.CompilerParams(vmem_limit_bytes=VMEM_LIMIT),
        cost_estimate=cost(len(partners), 6 + len(partners)),
        name=name,
    )(*operands)


def flags_of(pair_mask, reach):
    count = pair_mask.shape[0]
    me = lax.axis_index(BLK)
    block = lax.broadcasted_iota(jnp.int32, pair_mask.shape, 0)
    e = lax.broadcasted_iota(jnp.int32, pair_mask.shape, 1) - reach
    mine = jnp.sum(jnp.where(block == me, pair_mask, 0), axis=0)
    theirs = jnp.sum(jnp.where(block == lax.rem(me - e + count, count), pair_mask, 0), axis=0)
    return jnp.stack([mine, theirs])


def exchanged(values, axes):
    return lax.all_to_all(values, axes, 0, 0, tiled=True)


def totals(received, copies):
    return pl.pallas_call(
        total_kernel,
        out_shape=jax.ShapeDtypeStruct((copies, 1, 128), jnp.float32),
        in_specs=[VMEM],
        out_specs=VMEM,
        compiler_params=pltpu.CompilerParams(vmem_limit_bytes=VMEM_LIMIT),
        name="plane_total",
    )(received)


def after(value, *others):
    return lax.optimization_barrier((value, *others))[0]


def body(image_emb, text_emb, positives, pair_mask, log_scale, bias):
    reach = (pair_mask.shape[1] - 1) // 2
    scal = jnp.concatenate([jnp.exp(log_scale), bias])
    flags = flags_of(pair_mask, reach)

    def sent_on(held, *token):
        return [shifted(after(held[0], *token), BLK, 1), shifted(after(held[1], *token), BLK, -1)]

    def image_side(d, loss, acc, partners, raw=None, copies=0):
        which = [(0, reach + d), (0, reach - d)]
        return add_pairs(which, flags, scal, loss, image_half, acc, raw, partners[::-1], f"image_side_{d}", copies)

    def text_side(d, acc, partners, name, raw=None):
        which = [(1, reach - d), (1, reach + d)]
        return add_pairs(which, flags, scal, None, text_half, acc, raw, partners[::-1], f"text_side_{name}")[0]

    texts_1 = sent_on([text_emb, text_emb])
    images_1 = sent_on([image_emb, image_emb])
    image_half, text_half, image_acc, text_acc, loss_0 = own_pair(scal, positives, image_emb, text_emb)
    texts_2 = sent_on(texts_1, loss_0)
    image_acc, loss_1 = image_side(1, loss_0, image_acc, texts_1)
    images_2 = sent_on(images_1, loss_1)
    text_acc = text_side(1, text_acc, images_1, "1")
    texts_3 = sent_on(texts_2, text_acc)
    image_acc, loss_2 = image_side(2, loss_1, image_acc, texts_2)
    images_3 = sent_on(images_2, loss_2)
    text_acc = text_side(2, text_acc, images_2, "2")
    plane, line = ("x_hi", "y", "x_lo", "core"), ("z",)
    image_grad, losses = image_side(
        3, after(loss_2, text_acc), image_acc, texts_3, image_emb, lax.axis_size(plane)
    )
    sums = totals(exchanged(losses, plane), lax.axis_size(line))
    total = jnp.sum(exchanged(sums, line)[:, 0, 0]).reshape(1)
    text_grad = text_side(3, after(text_acc, sums), images_3, "3", text_emb)
    image_count = image_emb.shape[0] * lax.axis_size(ALL)
    return image_grad, text_grad, total / image_count


def solution(mesh):
    fine = Mesh(mesh.devices.reshape(2, 4, 16, 2, 2), ALL)
    rows = P(ALL, None)
    return jax.shard_map(
        body,
        mesh=fine,
        in_specs=(rows, rows, rows, P(), P(), P()),
        out_specs=(rows, rows, P()),
        check_vma=False,
    )
```

```python
import functools

import jax
import jax.numpy as jnp
from jax import lax
from jax.experimental import pallas as pl
from jax.experimental.pallas import tpu as pltpu
from jax.sharding import Mesh
from jax.sharding import PartitionSpec as P

ALL = ("x_hi", "y", "z", "x_lo", "core")
BLK = ("x_hi", "y", "z")

EPSILON = 1e-06
VMEM_LIMIT = 16 * 1024 * 1024


def shifted(value, axis, steps):
    count = lax.axis_size(axis)
    return lax.ppermute(value, axis, [(s, (s + steps) % count) for s in range(count)])


def dot(a, b, contract):
    return lax.dot_general(a, b, ((contract[:1], contract[1:]), ((), ())), preferred_element_type=jnp.float32)


def unit_of(raw):
    values = raw.astype(jnp.float32)
    inverse = lax.rsqrt(jnp.sum(values * values, axis=1, keepdims=True) + EPSILON)
    return values * inverse, inverse


def loss_and_sigmoid(u):
    small = jnp.exp(-jnp.abs(u))
    loss = jnp.maximum(u, 0.0) + jnp.log1p(small)
    return loss, jnp.where(u >= 0.0, 1.0, small) / (1.0 + small)


def grad_of(raw, upstream):
    unit, inverse = unit_of(raw)
    inward = jnp.sum(unit * upstream, axis=1, keepdims=True)
    return ((upstream - unit * inward) * inverse).astype(jnp.bfloat16)


def own_kernel(scal, positives, image, text, image_half, text_half, image_acc, text_acc, loss):
    image_half[...] = unit_of(image[...])[0].astype(jnp.bfloat16)
    text_half[...] = unit_of(text[...])[0].astype(jnp.bfloat16)
    z = scal[0] * dot(text_half[...], image_half[...], (1, 1)) + scal[1]
    match = lax.broadcasted_iota(jnp.int32, z.shape, 0) == positives[...]
    part, sigmoid = loss_and_sigmoid(jnp.where(match, -z, z))
    loss[0] = jnp.sum(part)
    slopes = (jnp.where(match, -sigmoid, sigmoid) * scal[0]).astype(jnp.bfloat16)
    text_acc[...] = dot(slopes, image_half[...], (1, 0))
    image_acc[...] = dot(slopes, text_half[...], (0, 0))


def pair_kernel(which, with_loss, last, flags, scal, *refs):
    refs = list(refs)
    loss_in = refs.pop(0) if with_loss else None
    half, acc = refs.pop(0), refs.pop(0)
    raw = refs.pop(0) if last else None
    partners = [refs.pop(0) for _ in which]
    out = refs.pop(0)
    loss_out = refs.pop(0) if with_loss else None
    total = refs.pop(0) if last else out
    loss = refs.pop(0) if with_loss and last else loss_out
    total[...] = acc[...]
    if with_loss:
        loss[0] = loss_in[0]
    for (row, column), partner in zip(which, partners):

        @pl.when(flags[row, column] > 0)
        def _(partner=partner):
            other = unit_of(partner[...])[0].astype(jnp.bfloat16)
            z = scal[0] * dot(half[...], other, (1, 1)) + scal[1]
            part, sigmoid = loss_and_sigmoid(z)
            if with_loss:
                loss[0] = loss[0] + jnp.sum(part)
            slopes = (sigmoid * scal[0]).astype(jnp.bfloat16)
            total[...] += dot(slopes, other, (1, 0))

    if last:
        out[...] = grad_of(raw[...], total[...])
        if with_loss:
            loss_out[...] = jnp.full(loss_out.shape, loss[0], jnp.float32)


def total_kernel(scale, received, out):
    out[...] = jnp.broadcast_to(scale * jnp.sum(received[...], axis=0, keepdims=True), out.shape)


SMEM = pl.BlockSpec(memory_space=pltpu.SMEM)
VMEM = pl.BlockSpec()


def cost(pairs, blocks):
    return pl.CostEstimate(flops=pairs * 4 * 384 * 384 * 1152, bytes_accessed=blocks * 384 * 1152 * 2, transcendentals=pairs * 3 * 384 * 384)


def own_pair(scal, positives, image, text):
    shape = image.shape
    return pl.pallas_call(
        own_kernel,
        out_shape=[jax.ShapeDtypeStruct(shape, jnp.bfloat16)] * 2 + [jax.ShapeDtypeStruct(shape, jnp.float32)] * 2 + [jax.ShapeDtypeStruct((1,), jnp.float32)],
        in_specs=[SMEM, VMEM, VMEM, VMEM],
        out_specs=[VMEM] * 4 + [SMEM],
        compiler_params=pltpu.CompilerParams(vmem_limit_bytes=VMEM_LIMIT),
        cost_estimate=cost(2, 8),
        name="own_pair",
    )(scal, positives, image, text)


def add_pairs(which, flags, scal, loss, half, acc, raw, partners, name, copies=0):
    with_loss, last = loss is not None, raw is not None
    operands = [flags, scal] + ([loss] if with_loss else []) + [half, acc] + ([raw] if last else []) + list(partners)
    in_specs = [SMEM, SMEM] + ([SMEM] if with_loss else []) + [VMEM] * (2 + last + len(partners))
    out_shape = [jax.ShapeDtypeStruct(acc.shape, jnp.bfloat16 if last else jnp.float32)]
    out_specs = [VMEM]
    if with_loss:
        out_shape.append(jax.ShapeDtypeStruct((copies, 1, 128) if last else (1,), jnp.float32))
        out_specs.append(VMEM if last else SMEM)
    aliases = {} if last else {3 + with_loss: 0}
    return pl.pallas_call(
        functools.partial(pair_kernel, tuple(which), with_loss, last),
        out_shape=out_shape,
        in_specs=in_specs,
        out_specs=out_specs,
        scratch_shapes=([pltpu.VMEM(acc.shape, jnp.float32)] + [pltpu.SMEM((1,), jnp.float32)] * with_loss) if last else [],
        input_output_aliases=aliases,
        compiler_params=pltpu.CompilerParams(vmem_limit_bytes=VMEM_LIMIT),
        cost_estimate=cost(len(partners), 6 + len(partners)),
        name=name,
    )(*operands)


def flags_of(pair_mask, reach):
    count = pair_mask.shape[0]
    me = lax.axis_index(BLK)
    block = lax.broadcasted_iota(jnp.int32, pair_mask.shape, 0)
    e = lax.broadcasted_iota(jnp.int32, pair_mask.shape, 1) - reach
    mine = jnp.sum(jnp.where(block == me, pair_mask, 0), axis=0)
    theirs = jnp.sum(jnp.where(block == lax.rem(me - e + count, count), pair_mask, 0), axis=0)
    return jnp.stack([mine, theirs])


def exchanged(values, axes):
    return lax.all_to_all(values, axes, 0, 0, tiled=True)


def totals(received, copies, scale):
    return pl.pallas_call(
        functools.partial(total_kernel, scale),
        out_shape=jax.ShapeDtypeStruct((copies, 1, 128), jnp.float32),
        in_specs=[VMEM],
        out_specs=VMEM,
        compiler_params=pltpu.CompilerParams(vmem_limit_bytes=VMEM_LIMIT),
        name="plane_total",
    )(received)


def after(value, *others):
    return lax.optimization_barrier((value, *others))[0]


def body(image_emb, text_emb, positives, pair_mask, log_scale, bias):
    reach = (pair_mask.shape[1] - 1) // 2
    scal = jnp.concatenate([jnp.exp(log_scale), bias])
    flags = flags_of(pair_mask, reach)

    def sent_on(held, *token):
        return [shifted(after(held[0], *token), BLK, 1), shifted(after(held[1], *token), BLK, -1)]

    def image_side(d, loss, acc, partners, raw=None, copies=0):
        which = [(0, reach + d), (0, reach - d)]
        return add_pairs(which, flags, scal, loss, image_half, acc, raw, partners[::-1], f"image_side_{d}", copies)

    def text_side(d, acc, partners, name, raw=None):
        which = [(1, reach - d), (1, reach + d)]
        return add_pairs(which, flags, scal, None, text_half, acc, raw, partners[::-1], f"text_side_{name}")[0]

    texts_1 = sent_on([text_emb, text_emb])
    images_1 = sent_on([image_emb, image_emb])
    image_half, text_half, image_acc, text_acc, loss_0 = own_pair(scal, positives, image_emb, text_emb)
    texts_2 = sent_on(texts_1, loss_0)
    image_acc, loss_1 = image_side(1, loss_0, image_acc, texts_1)
    images_2 = sent_on(images_1, loss_1)
    text_acc = text_side(1, text_acc, images_1, "1")
    texts_3 = sent_on(texts_2, text_acc)
    image_acc, loss_2 = image_side(2, loss_1, image_acc, texts_2)
    images_3 = sent_on(images_2, loss_2)
    text_acc = text_side(2, text_acc, images_2, "2")
    plane, line = ("x_hi", "y", "x_lo", "core"), ("z",)
    image_grad, losses = image_side(
        3, after(loss_2, text_acc), image_acc, texts_3, image_emb, lax.axis_size(plane)
    )
    images = image_emb.shape[0] * lax.axis_size(ALL)
    sums = totals(exchanged(losses, plane), lax.axis_size(line), 1.0 / images)
    total = jnp.sum(exchanged(sums, line)[:, 0, 0]).reshape(1)
    text_grad = text_side(3, after(text_acc, sums), images_3, "3", text_emb)
    return image_grad, text_grad, total


def solution(mesh):
    fine = Mesh(mesh.devices.reshape(2, 4, 16, 2, 2), ALL)
    rows = P(ALL, None)
    return jax.shard_map(
        body,
        mesh=fine,
        in_specs=(rows, rows, rows, P(), P(), P()),
        out_specs=(rows, rows, P()),
        check_vma=False,
    )
```

```python
import functools

import jax
import jax.numpy as jnp
from jax import lax
from jax.experimental import pallas as pl
from jax.experimental.pallas import tpu as pltpu
from jax.sharding import Mesh
from jax.sharding import PartitionSpec as P

ALL = ("x_hi", "y", "z", "x_lo", "core")
BLK = ("x_hi", "y", "z")

EPSILON = 1e-06
VMEM_LIMIT = 16 * 1024 * 1024


def shifted(value, axis, steps):
    count = lax.axis_size(axis)
    return lax.ppermute(value, axis, [(s, (s + steps) % count) for s in range(count)])


def dot(a, b, contract):
    return lax.dot_general(a, b, ((contract[:1], contract[1:]), ((), ())), preferred_element_type=jnp.float32)


def unit_of(raw):
    values = raw.astype(jnp.float32)
    inverse = lax.rsqrt(jnp.sum(values * values, axis=1, keepdims=True) + EPSILON)
    return values * inverse, inverse


def loss_and_sigmoid(u):
    small = jnp.exp(-jnp.abs(u))
    loss = jnp.maximum(u, 0.0) + jnp.log1p(small)
    return loss, jnp.where(u >= 0.0, 1.0, small) / (1.0 + small)


def grad_of(raw, upstream):
    unit, inverse = unit_of(raw)
    inward = jnp.sum(unit * upstream, axis=1, keepdims=True)
    return ((upstream - unit * inward) * inverse).astype(jnp.bfloat16)


def own_kernel(scal, positives, image, text, image_half, text_half, image_acc, text_acc, loss):
    image_half[...] = unit_of(image[...])[0].astype(jnp.bfloat16)
    text_half[...] = unit_of(text[...])[0].astype(jnp.bfloat16)
    z = scal[0] * dot(text_half[...], image_half[...], (1, 1)) + scal[1]
    match = lax.broadcasted_iota(jnp.int32, z.shape, 0) == positives[...]
    part, sigmoid = loss_and_sigmoid(jnp.where(match, -z, z))
    loss[0] = jnp.sum(part)
    slopes = (jnp.where(match, -sigmoid, sigmoid) * scal[0]).astype(jnp.bfloat16)
    text_acc[...] = dot(slopes, image_half[...], (1, 0))
    image_acc[...] = dot(slopes, text_half[...], (0, 0))


def pair_kernel(which, with_loss, last, flags, scal, *refs):
    refs = list(refs)
    loss_in = refs.pop(0) if with_loss else None
    half, acc = refs.pop(0), refs.pop(0)
    raw = refs.pop(0) if last else None
    partners = [refs.pop(0) for _ in which]
    out = refs.pop(0)
    loss_out = refs.pop(0) if with_loss else None
    total = refs.pop(0) if last else out
    loss = refs.pop(0) if with_loss and last else loss_out
    if with_loss:
        loss[0] = loss_in[0]
    so_far = acc
    for (row, column), partner in zip(which, partners):
        scored = flags[row, column] > 0

        @pl.when(scored)
        def _(partner=partner, so_far=so_far):
            other = unit_of(partner[...])[0].astype(jnp.bfloat16)
            z = scal[0] * dot(half[...], other, (1, 1)) + scal[1]
            part, sigmoid = loss_and_sigmoid(z)
            if with_loss:
                loss[0] = loss[0] + jnp.sum(part)
            slopes = (sigmoid * scal[0]).astype(jnp.bfloat16)
            total[...] = so_far[...] + dot(slopes, other, (1, 0))

        if so_far is acc:

            @pl.when(jnp.logical_not(scored))
            def _():
                total[...] = acc[...]

        so_far = total

    if last:
        out[...] = grad_of(raw[...], total[...])
        if with_loss:
            loss_out[...] = jnp.full(loss_out.shape, loss[0], jnp.float32)


def total_kernel(scale, received, out):
    out[...] = jnp.broadcast_to(scale * jnp.sum(received[...], axis=0, keepdims=True), out.shape)


SMEM = pl.BlockSpec(memory_space=pltpu.SMEM)
VMEM = pl.BlockSpec()


def cost(pairs, blocks):
    return pl.CostEstimate(flops=pairs * 4 * 384 * 384 * 1152, bytes_accessed=blocks * 384 * 1152 * 2, transcendentals=pairs * 3 * 384 * 384)


def own_pair(scal, positives, image, text):
    shape = image.shape
    return pl.pallas_call(
        own_kernel,
        out_shape=[jax.ShapeDtypeStruct(shape, jnp.bfloat16)] * 2 + [jax.ShapeDtypeStruct(shape, jnp.float32)] * 2 + [jax.ShapeDtypeStruct((1,), jnp.float32)],
        in_specs=[SMEM, VMEM, VMEM, VMEM],
        out_specs=[VMEM] * 4 + [SMEM],
        compiler_params=pltpu.CompilerParams(vmem_limit_bytes=VMEM_LIMIT),
        cost_estimate=cost(2, 8),
        name="own_pair",
    )(scal, positives, image, text)


def add_pairs(which, flags, scal, loss, half, acc, raw, partners, name, copies=0):
    with_loss, last = loss is not None, raw is not None
    operands = [flags, scal] + ([loss] if with_loss else []) + [half, acc] + ([raw] if last else []) + list(partners)
    in_specs = [SMEM, SMEM] + ([SMEM] if with_loss else []) + [VMEM] * (2 + last + len(partners))
    out_shape = [jax.ShapeDtypeStruct(acc.shape, jnp.bfloat16 if last else jnp.float32)]
    out_specs = [VMEM]
    if with_loss:
        out_shape.append(jax.ShapeDtypeStruct((copies, 1, 128) if last else (1,), jnp.float32))
        out_specs.append(VMEM if last else SMEM)
    aliases = {} if last else {3 + with_loss: 0}
    return pl.pallas_call(
        functools.partial(pair_kernel, tuple(which), with_loss, last),
        out_shape=out_shape,
        in_specs=in_specs,
        out_specs=out_specs,
        scratch_shapes=([pltpu.VMEM(acc.shape, jnp.float32)] + [pltpu.SMEM((1,), jnp.float32)] * with_loss) if last else [],
        input_output_aliases=aliases,
        compiler_params=pltpu.CompilerParams(vmem_limit_bytes=VMEM_LIMIT),
        cost_estimate=cost(len(partners), 6 + len(partners)),
        name=name,
    )(*operands)


def flags_of(pair_mask, reach):
    count = pair_mask.shape[0]
    me = lax.axis_index(BLK)
    block = lax.broadcasted_iota(jnp.int32, pair_mask.shape, 0)
    e = lax.broadcasted_iota(jnp.int32, pair_mask.shape, 1) - reach
    mine = jnp.sum(jnp.where(block == me, pair_mask, 0), axis=0)
    theirs = jnp.sum(jnp.where(block == lax.rem(me - e + count, count), pair_mask, 0), axis=0)
    return jnp.stack([mine, theirs])


def exchanged(values, axes):
    return lax.all_to_all(values, axes, 0, 0, tiled=True)


def totals(received, copies, scale):
    return pl.pallas_call(
        functools.partial(total_kernel, scale),
        out_shape=jax.ShapeDtypeStruct((copies, 1, 128), jnp.float32),
        in_specs=[VMEM],
        out_specs=VMEM,
        compiler_params=pltpu.CompilerParams(vmem_limit_bytes=VMEM_LIMIT),
        name="plane_total",
    )(received)


def after(value, *others):
    return lax.optimization_barrier((value, *others))[0]


def body(image_emb, text_emb, positives, pair_mask, log_scale, bias):
    reach = (pair_mask.shape[1] - 1) // 2
    scal = jnp.concatenate([jnp.exp(log_scale), bias])
    flags = flags_of(pair_mask, reach)

    def sent_on(held, *token):
        return [shifted(after(held[0], *token), BLK, 1), shifted(after(held[1], *token), BLK, -1)]

    def image_side(d, loss, acc, partners, raw=None, copies=0):
        which = [(0, reach + d), (0, reach - d)]
        return add_pairs(which, flags, scal, loss, image_half, acc, raw, partners[::-1], f"image_side_{d}", copies)

    def text_side(d, acc, partners, name, raw=None):
        which = [(1, reach - d), (1, reach + d)]
        return add_pairs(which, flags, scal, None, text_half, acc, raw, partners[::-1], f"text_side_{name}")[0]

    texts_1 = sent_on([text_emb, text_emb])
    images_1 = sent_on([image_emb, image_emb])
    image_half, text_half, image_acc, text_acc, loss_0 = own_pair(scal, positives, image_emb, text_emb)
    texts_2 = sent_on(texts_1, loss_0)
    image_acc, loss_1 = image_side(1, loss_0, image_acc, texts_1)
    images_2 = sent_on(images_1, loss_1)
    text_acc = text_side(1, text_acc, images_1, "1")
    texts_3 = sent_on(texts_2, text_acc)
    image_acc, loss_2 = image_side(2, loss_1, image_acc, texts_2)
    images_3 = sent_on(images_2, loss_2)
    text_acc = text_side(2, text_acc, images_2, "2")
    plane, line = ("x_hi", "y", "x_lo", "core"), ("z",)
    image_grad, losses = image_side(
        3, after(loss_2, text_acc), image_acc, texts_3, image_emb, lax.axis_size(plane)
    )
    images = image_emb.shape[0] * lax.axis_size(ALL)
    sums = totals(exchanged(losses, plane), lax.axis_size(line), 1.0 / images)
    total = jnp.sum(exchanged(sums, line)[:, 0, 0]).reshape(1)
    text_grad = text_side(3, after(text_acc, sums), images_3, "3", text_emb)
    return image_grad, text_grad, total


def solution(mesh):
    fine = Mesh(mesh.devices.reshape(2, 4, 16, 2, 2), ALL)
    rows = P(ALL, None)
    return jax.shard_map(
        body,
        mesh=fine,
        in_specs=(rows, rows, rows, P(), P(), P()),
        out_specs=(rows, rows, P()),
        check_vma=False,
    )
```
